32 devices in a mesh: groups: 2 (over y), slab: 4 (over x, core), head: 4 (over z).
Axes of the slice: x: 2, y: 2, z: 4, core: 2. Of those that a mesh axis runs over, the one named last changes fastest.
Arguments:
- query_rows: bfloat16 [2048, 5120], P(('groups', 'slab', 'head')), parts along dimension 0, may hold values from -16 to 16
- key_rows: bfloat16 [2048, 5120], P(('groups', 'slab', 'head')), parts along dimension 0, may hold values from -16 to 16
- value_rows: bfloat16 [2048, 5120], P(('groups', 'slab', 'head')), parts along dimension 0, may hold values from -4 to 4
- tile_mask: int32 [40, 16, 5], P(None, ('groups', 'slab')), parts along dimension 1, may hold values from 0 to 1, as said below
- head_slot: int32 [40], replicated, may hold values from 0 to 39, as said below
Outputs:
- attended: bfloat16 [2048, 5120], P(('groups', 'slab', 'head')), parts along dimension 0
- slot_lse: float32 [40, 2048], P('head', ('groups', 'slab')), parts along dimension 1
The draws below stay inside these ranges and needn't reach their ends.
There are 2 independent parts, one for each index of `groups`. The reference program is written for one: setup_inputs(seed, part) draws one part's arguments, and reference() takes and returns one part's arrays. A program takes and returns all parts, laid end to end along the dimension named above; an argument that names none is the same for every part. Nothing has to cross between parts.
Inputs may be any that keep to these rules, and one draw needn't show every extreme that they name: `tile_mask`: entry 2 of every row of every head is 1. `head_slot`: distinct; slots o * 10 to o * 10 + 9 belong to owner o along the head axis; every owner holds at most 10 heads and some owner holds 10.
All inputs are finite; a program needn't handle non-finite values.
Results may differ from the reference program's by a relative error of at most 0.0045.
Values may be sent and summed in bfloat16 or wider, within the bound.
No kernel may reach another device: no remote copies, remote signals or barrier semaphores. Data moves between devices by JAX's collectives and lax.ppermute only.
A program may use at most 64 MiB of HBM per device.

```python
import jax
import jax.numpy as jnp
from jax import lax

HEADS = 40
DH = 128
D = 5120
BLK = 128
REACH = 2
BAND = 5
HALO = 256
TOKENS = 1024
NBLK = 8
CAP = 10
SLOTS = 40


def paired_rows(key):
    base = jax.random.fold_in(key, 7)
    query_base = jnp.clip(jax.random.normal(jax.random.fold_in(base, 1), (TOKENS, D), jnp.float32), -4.0, 4.0)
    key_base = jnp.clip(jax.random.normal(jax.random.fold_in(base, 2), (TOKENS, D), jnp.float32), -4.0, 4.0)
    return (query_base, key_base)


def draw_query_rows(key, part):
    return paired_rows(key)[0].astype(jnp.bfloat16)


def draw_key_rows(key, part):
    return paired_rows(key)[1].astype(jnp.bfloat16)


def draw_tile_mask(key, part):
    first = jax.random.fold_in(key, 21)
    levels = jax.random.randint(jax.random.fold_in(first, 1), (HEADS, 1, 1), 3, 11)
    votes = jax.random.randint(jax.random.fold_in(first, 2), (HEADS, NBLK, BAND), 0, 10)
    column = jnp.arange(BAND, dtype=jnp.int32)[None, None, :]
    return jnp.where(column == REACH, 1, (votes < levels).astype(jnp.int32)).astype(jnp.int32)


def draw_head_slot(key, part):
    first = jax.random.fold_in(key, 33)
    owners = SLOTS // CAP
    base_count = HEADS // owners
    extra = HEADS - base_count * owners
    order = jax.random.permutation(jax.random.fold_in(first, 1), owners)
    ranks = jnp.argsort(order, stable=True).astype(jnp.int32)
    counts = base_count + (ranks < extra).astype(jnp.int32)
    slot_ids = jnp.arange(SLOTS, dtype=jnp.int32)
    used = slot_ids % CAP < counts[slot_ids // CAP]
    used_first = jnp.argsort(1 - used.astype(jnp.int32), stable=True).astype(jnp.int32)[:HEADS]
    shuffle = jax.random.permutation(jax.random.fold_in(first, 2), HEADS)
    return used_first[shuffle].astype(jnp.int32)


def block_levels(rng, extent, cuts, least, largest):
    gain = 1.0
    for axis_at, blocks in cuts:
        draws = jax.random.uniform(jax.random.fold_in(jax.random.fold_in(rng, 6), axis_at), (blocks,), jnp.float32, least / len(cuts), largest / len(cuts))
        gain = gain * jnp.repeat(jnp.exp(draws), extent[axis_at] // blocks).reshape((-1,) + (1,) * (len(extent) - 1 - axis_at))
    return gain


def centred(rng, extent, spread, limit, split=(), kind=jnp.bfloat16):
    entries = spread * jax.random.normal(rng, extent, jnp.float32)
    if split:
        entries = entries * block_levels(rng, extent, split, -0.22, 0.18)
    return jnp.clip(entries, -limit, limit).astype(kind)


def setup_inputs(seed: int = 0, part: int = 0) -> dict:
    keys = jax.random.split(jax.random.key(seed), 6)
    part_splits = jax.random.split(jax.random.fold_in(keys[5], part), 6)
    query_rows = draw_query_rows(jax.random.fold_in(jax.random.fold_in(keys[5], part), 71), part)
    key_rows = draw_key_rows(jax.random.fold_in(jax.random.fold_in(keys[5], part), 71), part)
    value_rows = centred(part_splits[2], (TOKENS, D), 1.0, 4.0, ((0, 16),))
    tile_mask = draw_tile_mask(jax.random.fold_in(jax.random.fold_in(keys[5], part), 71), part)
    head_slot = draw_head_slot(jax.random.fold_in(keys[5], 71), part)
    return {"query_rows": query_rows, "key_rows": key_rows, "value_rows": value_rows, "tile_mask": tile_mask, "head_slot": head_slot}


def reference(query_rows, key_rows, value_rows, tile_mask, head_slot):
    scale = DH ** -0.5
    head_queries = query_rows.reshape(TOKENS, HEADS, DH).transpose(1, 0, 2)
    head_keys = jnp.pad(key_rows.reshape(TOKENS, HEADS, DH).transpose(1, 0, 2), ((0, 0), (HALO, HALO), (0, 0)))
    head_values = jnp.pad(value_rows.reshape(TOKENS, HEADS, DH).transpose(1, 0, 2), ((0, 0), (HALO, HALO), (0, 0)))

    def one_head(head_args):
        queries, keys_ext, values_ext, head_mask = head_args

        def one_tile(block):
            start = (block * BLK).astype(jnp.int32)
            rows_query = lax.dynamic_slice_in_dim(queries, start, BLK, 0)
            window_keys = lax.dynamic_slice_in_dim(keys_ext, start, BAND * BLK, 0)
            window_values = lax.dynamic_slice_in_dim(values_ext, start, BAND * BLK, 0)
            scores = jnp.dot(rows_query, window_keys.T, preferred_element_type=jnp.float32) * scale
            targets = block - REACH + jnp.arange(BAND, dtype=jnp.int32)
            allowed = (head_mask[block] > 0) & (targets >= 0) & (targets < NBLK)
            allowed_full = jnp.repeat(allowed, BLK)
            masked = jnp.where(allowed_full[None, :], scores, -1e30)
            highest = jnp.max(masked, axis=1, keepdims=True)
            weights = jnp.exp(masked - highest)
            total = jnp.sum(weights, axis=1)
            summed = jnp.dot(weights.astype(jnp.bfloat16), window_values, preferred_element_type=jnp.float32)
            result = (summed / total[:, None]).astype(jnp.bfloat16)
            return result, highest[:, 0] + jnp.log(total)

        tiles_out, tiles_lse = jax.vmap(one_tile)(jnp.arange(NBLK, dtype=jnp.int32))
        return tiles_out.reshape(TOKENS, DH), tiles_lse.reshape(TOKENS)

    head_out, head_lse = lax.map(one_head, (head_queries, head_keys, head_values, tile_mask))
    attended = head_out.transpose(1, 0, 2).reshape(TOKENS, HEADS * DH)
    slot_ids = jnp.arange(SLOTS, dtype=jnp.int32)
    placed = (head_slot[None, :] == slot_ids[:, None]).astype(jnp.float32)
    slot_lse = jnp.dot(placed, head_lse, precision=lax.Precision.HIGHEST)
    return attended, slot_lse
```

```python
import functools
import math

import jax
import jax.numpy as jnp
from jax import lax
from jax.experimental import pallas as pl
from jax.experimental.pallas import tpu as pltpu
from jax.sharding import PartitionSpec as P

VMEM_BYTES = 24 * 1024 * 1024
ANY = pl.BlockSpec(memory_space=pl.ANY)
SMEM = pl.BlockSpec(memory_space=pltpu.SMEM)
VMEM = pl.BlockSpec(memory_space=pltpu.VMEM)


def params(aliasing=False):
    return pltpu.CompilerParams(vmem_limit_bytes=VMEM_BYTES)


def invert(head_slot, head_of):
    for j in range(head_of.shape[0]):
        head_of[j] = 0
    for h in range(head_slot.shape[0]):
        head_of[head_slot[h]] = h


def pack_kernel(owners, capacity, first, count, dim, sources, head_slot, *refs):
    rows = refs[:sources]
    outs = refs[sources : sources + owners]
    head_of, sem = refs[sources + owners :]
    me = lax.axis_index("head")
    invert(head_slot, head_of)
    copies = []
    for k in range(owners):
        owner = lax.rem(me + k, owners)
        for c in range(count):
            head = head_of[owner * capacity + first + c]
            columns = pl.ds(pl.multiple_of(head * dim, dim), dim)
            for s in range(sources):
                copies.append(
                    pltpu.make_async_copy(
                        rows[s].at[:, columns], outs[k].at[s, c], sem.at[len(copies)]
                    )
                )
                copies[-1].start()
    for copy in copies:
        copy.wait()


def pack(head_slot, rows, owners, capacity, first, count, heads):
    tokens, width = rows[0].shape
    dim = width // heads
    shape = jax.ShapeDtypeStruct((len(rows), count, tokens, dim), rows[0].dtype)
    nbytes = 2 * owners * math.prod(shape.shape) * 2
    return pl.pallas_call(
        functools.partial(pack_kernel, owners, capacity, first, count, dim, len(rows)),
        out_shape=[shape] * owners,
        in_specs=[SMEM] + [ANY] * len(rows),
        out_specs=[ANY] * owners,
        scratch_shapes=[
            pltpu.SMEM((owners * capacity,), jnp.int32),
            pltpu.SemaphoreType.DMA((owners * count * len(rows),)),
        ],
        compiler_params=params(),
        cost_estimate=pl.CostEstimate(flops=0, bytes_accessed=nbytes, transcendentals=0),
        name="pack",
    )(head_slot, *rows)


def join_kernel(owners, *refs):
    blocks, out, sem = refs[:owners], refs[owners], refs[owners + 1]
    me = lax.axis_index("head")
    tokens = blocks[0].shape[2]
    copies = []
    for k in range(owners):
        start = lax.rem(me - k + owners, owners) * tokens
        place = pl.ds(pl.multiple_of(start, tokens), tokens)
        copies.append(pltpu.make_async_copy(blocks[k], out.at[:, :, place], sem.at[k]))
        copies[-1].start()
    for copy in copies:
        copy.wait()


def join(blocks):
    owners = len(blocks)
    s, c, t, d = blocks[0].shape
    shape = jax.ShapeDtypeStruct((s, c, t * owners, d), blocks[0].dtype)
    return pl.pallas_call(
        functools.partial(join_kernel, owners),
        out_shape=shape,
        in_specs=[ANY] * owners,
        out_specs=ANY,
        scratch_shapes=[pltpu.SemaphoreType.DMA((owners,))],
        compiler_params=params(),
        cost_estimate=pl.CostEstimate(
            flops=0, bytes_accessed=4 * math.prod(shape.shape), transcendentals=0
        ),
        name="join",
    )(*blocks)


def attend_kernel(owners, capacity, first, tiles, tiles_all, band, head_slot, mask, *refs):
    q_blocks = refs[:owners]
    mid, before, after = refs[owners : owners + 3]
    outs = refs[owners + 3 : 2 * owners + 3]
    lse_ref, q_all, o_all, head_of, used = refs[2 * owners + 3 :]
    me = lax.axis_index("head")
    tile_base = lax.axis_index("slab") * tiles
    _, count, tok, dim = q_blocks[0].shape
    reach = (band - 1) // 2
    rows = tok * owners // tiles
    scale = dim ** (-0.5)
    base2 = scale * math.log2(math.e)

    for j in range(owners * capacity):
        head_of[j] = 0
        used[j] = 0
    for h in range(head_slot.shape[0]):
        head_of[head_slot[h]] = h
        used[head_slot[h]] = 1

    for k in range(owners):
        place = pl.ds(pl.multiple_of(lax.rem(me - k + owners, owners) * tok, tok), tok)
        q_all[:, place, :] = q_blocks[k][0]

    def window(which, c, first_tile):
        parts = []
        low, high = first_tile * rows, (first_tile + band) * rows
        halo, own = reach * rows, tiles * rows
        if low < halo:
            parts.append(before[which, c, low : min(high, halo)])
        if low < halo + own and high > halo:
            parts.append(mid[which, c, max(low - halo, 0) : min(high - halo, own)])
        if high > halo + own:
            parts.append(after[which, c, max(low - halo - own, 0) : high - halo - own])
        return jnp.concatenate(parts, axis=0) if len(parts) > 1 else parts[0]

    for c in range(count):
        slot = me * capacity + first + c
        head = head_of[slot]
        valid = used[slot] > 0
        for t in range(tiles):
            queries = q_all[c, t * rows : (t + 1) * rows, :]
            scores = lax.dot_general(
                queries,
                window(0, c, t),
                (((1,), (1,)), ((), ())),
                preferred_element_type=jnp.float32,
            )
            kept = []
            for b in range(band):
                tile = tile_base + t + b - reach
                flag = mask[(head * tiles + t) * band + b]
                allowed = (flag > 0) & (tile >= 0) & (tile < tiles_all)
                part = scores[:, b * rows : (b + 1) * rows]
                kept.append(jnp.where(allowed, part, -1e30))
            masked = jnp.concatenate(kept, axis=1)
            highest = jnp.max(masked, axis=1, keepdims=True)
            weights = jnp.exp2((masked - highest) * base2)
            total = jnp.sum(weights, axis=1, keepdims=True)
            summed = jnp.dot(
                weights.astype(jnp.bfloat16), window(1, c, t), preferred_element_type=jnp.float32
            )
            o_all[c, t * rows : (t + 1) * rows, :] = (summed / total).astype(jnp.bfloat16)
            lse = jnp.where(valid, highest * scale + jnp.log(total), 0.0)
            lse_ref[c : c + 1, t * rows : (t + 1) * rows] = jnp.transpose(
                jnp.broadcast_to(lse, (rows, 128))
            )[0:1, :]

    for k in range(owners):
        place = pl.ds(pl.multiple_of(lax.rem(me + k, owners) * tok, tok), tok)
        outs[k][...] = o_all[:, place, :]


def attend(head_slot, mask, q_blocks, mid, before, after, capacity, first, tiles, tiles_all, band):
    owners = len(q_blocks)
    _, count, tok, dim = q_blocks[0].shape
    out = jax.ShapeDtypeStruct((count, tok, dim), jnp.bfloat16)
    keys = band * (tok * owners // tiles)
    pairs = count * tok * owners * keys
    return pl.pallas_call(
        functools.partial(attend_kernel, owners, capacity, first, tiles, tiles_all, band),
        out_shape=[out] * owners + [jax.ShapeDtypeStruct((count, tok * owners), jnp.float32)],
        in_specs=[SMEM, SMEM] + [VMEM] * (owners + 3),
        out_specs=[VMEM] * (owners + 1),
        scratch_shapes=[
            pltpu.VMEM((count, tok * owners, dim), jnp.bfloat16),
            pltpu.VMEM((count, tok * owners, dim), jnp.bfloat16),
            pltpu.SMEM((owners * capacity,), jnp.int32),
            pltpu.SMEM((owners * capacity,), jnp.int32),
        ],
        compiler_params=params(),
        cost_estimate=pl.CostEstimate(
            flops=4 * pairs * dim,
            bytes_accessed=4 * math.prod(mid.shape) + 4 * math.prod(before.shape),
            transcendentals=pairs,
        ),
        name="attend",
    )(head_slot, mask, *q_blocks, mid, before, after)


def unpack_kernel(owners, capacity, first, count, dim, head_slot, *refs):
    blocks = refs[:owners]
    out, head_of, used, sem = refs[-4:]
    me = lax.axis_index("head")
    for j in range(owners * capacity):
        head_of[j] = 0
        used[j] = 0
    for h in range(head_slot.shape[0]):
        head_of[head_slot[h]] = h
        used[head_slot[h]] = 1

    def each(act):
        for k in range(owners):
            owner = lax.rem(me - k + owners, owners)
            for c in range(count):
                slot = owner * capacity + first + c
                columns = pl.ds(pl.multiple_of(head_of[slot] * dim, dim), dim)
                copy = pltpu.make_async_copy(
                    blocks[k].at[c], out.at[:, columns], sem.at[k * count + c]
                )
                pl.when(used[slot] > 0)(functools.partial(act, copy))

    each(lambda copy: copy.start())
    each(lambda copy: copy.wait())


def unpack(head_slot, blocks, target, capacity, first, shape):
    owners = len(blocks)
    count, tok, dim = blocks[0].shape
    operands = list(blocks) + ([] if target is None else [target])
    return pl.pallas_call(
        functools.partial(unpack_kernel, owners, capacity, first, count, dim),
        out_shape=shape,
        in_specs=[SMEM] + [ANY] * len(operands),
        out_specs=ANY,
        input_output_aliases={} if target is None else {owners + 1: 0},
        scratch_shapes=[
            pltpu.SMEM((owners * capacity,), jnp.int32),
            pltpu.SMEM((owners * capacity,), jnp.int32),
            pltpu.SemaphoreType.DMA((owners * count,)),
        ],
        compiler_params=params(),
        cost_estimate=pl.CostEstimate(
            flops=0, bytes_accessed=4 * owners * count * tok * dim, transcendentals=0
        ),
        name="unpack",
    )(head_slot, *operands)


def exchange(blocks):
    owners = len(blocks)
    return [blocks[0]] + [
        lax.ppermute(blocks[k], "head", [(i, (i + k) % owners) for i in range(owners)])
        for k in range(1, owners)
    ]


def on_device(query_rows, key_rows, value_rows, tile_mask, head_slot):
    owners = lax.axis_size("head")
    slabs = lax.axis_size("slab")
    tok_dev = query_rows.shape[0]
    heads, tiles, band = tile_mask.shape
    capacity = (heads + owners - 1) // owners
    reach = (band - 1) // 2
    tok_slab = tok_dev * owners
    halo = reach * (tok_slab // tiles)
    mask = tile_mask.reshape(-1)
    half = (capacity + 1) // 2
    groups = [(0, half), (half, capacity - half)]
    groups = [g for g in groups if g[1]]
    up = [(i, i + 1) for i in range(slabs - 1)]
    down = [(j, i) for i, j in up]

    args = (owners, capacity)
    pairs = []
    for first, count in groups:
        packed = pack(head_slot, (key_rows, value_rows), *args, first, count, heads)
        mid = join(exchange(packed))
        last = lax.slice_in_dim(mid, tok_slab - halo, tok_slab, axis=2)
        lead = lax.slice_in_dim(mid, 0, halo, axis=2)
        before = lax.ppermute(last, "slab", up)
        after = lax.ppermute(lead, "slab", down)
        pairs.append((mid, before, after))
    queries = [
        exchange(pack(head_slot, (query_rows,), *args, first, count, heads))
        for first, count in groups
    ]
    target, lses = None, []
    for (first, count), pair, q_blocks in zip(groups, pairs, queries):
        *outs, lse = attend(
            head_slot, mask, q_blocks, *pair, capacity, first, tiles, tiles * slabs, band
        )
        lses.append(lse)
        target = unpack(
            head_slot,
            exchange(outs),
            target,
            capacity,
            first,
            jax.ShapeDtypeStruct(query_rows.shape, query_rows.dtype),
        )
    return target, jnp.concatenate(lses, axis=0)


def solution(mesh):
    rows = P(("groups", "slab", "head"), None)
    in_specs = (rows, rows, rows, P(None, ("groups", "slab"), None), P())
    out_specs = (rows, P("head", ("groups", "slab")))
    return jax.shard_map(
        on_device, mesh=mesh, in_specs=in_specs, out_specs=out_specs, check_vma=False
    )
```

```python
import functools
import math

import jax
import jax.numpy as jnp
from jax import lax
from jax.experimental import pallas as pl
from jax.experimental.pallas import tpu as pltpu
from jax.sharding import PartitionSpec as P

HBM = pl.BlockSpec(memory_space=pltpu.HBM)
ANY = pl.BlockSpec(memory_space=pl.ANY)
SMEM = pl.BlockSpec(memory_space=pltpu.SMEM)
VMEM = pl.BlockSpec(memory_space=pltpu.VMEM)
SMALL = pltpu.CompilerParams(vmem_limit_bytes=4 * 1024 * 1024)
LARGE = pltpu.CompilerParams(vmem_limit_bytes=16 * 1024 * 1024)


def in_hbm(x):
    return pltpu.with_memory_space_constraint(x, pltpu.HBM)


def cost(nbytes, flops=0, transcendentals=0):
    return pl.CostEstimate(flops=flops, bytes_accessed=nbytes, transcendentals=transcendentals)


def invert(head_slot, head_of, used=None):
    for j in range(head_of.shape[0]):
        head_of[j] = 0
        if used is not None:
            used[j] = 0
    for h in range(head_slot.shape[0]):
        head_of[head_slot[h]] = h
        if used is not None:
            used[head_slot[h]] = 1


def pack_kernel(owners, capacity, dim, parts, sources, waited, head_slot, *refs):
    rows = refs[:sources]
    outs = refs[sources + waited : sources + waited + owners]
    held = refs[sources + waited + owners : 2 * sources + waited + owners]
    slots, head_of, sem, sem_slots = refs[2 * sources + waited + owners :]
    me = lax.axis_index("head")
    slot_copy = pltpu.make_async_copy(head_slot, slots, sem_slots)
    slot_copy.start()
    chunks = sem.shape[1]
    size = rows[0].shape[0] // chunks
    copies = []
    for i in range(sources):
        for j in range(chunks):
            place = pl.ds(j * size, size)
            copies.append(
                pltpu.make_async_copy(rows[i].at[place], held[i].at[place], sem.at[i, j])
            )
            copies[-1].start()
    slot_copy.wait()
    invert(slots, head_of)
    for copy in copies:
        copy.wait()
    for k in range(owners):
        owner = lax.rem(me + k, owners)
        place = 0
        for source, first, count in parts:
            for c in range(count):
                head = head_of[owner * capacity + first + c]
                columns = pl.ds(pl.multiple_of(head * dim, dim), dim)
                outs[k][place] = held[source][:, columns]
                place += 1


def pack(head_slot, parts, owners, capacity, dim, after=()):
    rows = [row for row, _, _ in parts]
    total = sum(count for _, _, count in parts)
    tokens = rows[0].shape[0]
    shape = jax.ShapeDtypeStruct((total, tokens, dim), rows[0].dtype)
    places = tuple((i, first, count) for i, (_, first, count) in enumerate(parts))
    chunks = max(tokens // 16, 1)
    return pl.pallas_call(
        functools.partial(pack_kernel, owners, capacity, dim, places, len(rows), len(after)),
        out_shape=[shape] * owners,
        in_specs=[ANY] * (1 + len(rows) + len(after)),
        out_specs=[VMEM] * owners,
        scratch_shapes=[pltpu.VMEM(row.shape, row.dtype) for row in rows]
        + [
            pltpu.SMEM(head_slot.shape, jnp.int32),
            pltpu.SMEM((owners * capacity,), jnp.int32),
            pltpu.SemaphoreType.DMA((len(rows), chunks)),
            pltpu.SemaphoreType.DMA,
        ],
        cost_estimate=cost(4 * owners * math.prod(shape.shape)),
        compiler_params=SMALL,
        name="pack",
    )(*[in_hbm(x) for x in (head_slot, *rows)], *after)


def join_kernel(owners, count, *refs):
    blocks, out, sem = refs[:owners], refs[owners], refs[owners + 1]
    me = lax.axis_index("head")
    tokens = blocks[0].shape[1]
    copies = []
    for k in range(owners):
        start = lax.rem(me - k + owners, owners) * tokens
        place = pl.ds(pl.multiple_of(start, tokens), tokens)
        copies.append(
            pltpu.make_async_copy(blocks[k].at[pl.ds(0, count)], out.at[:, place], sem.at[k])
        )
        copies[-1].start()
    for copy in copies:
        copy.wait()


def join(blocks, count):
    owners = len(blocks)
    _, t, d = blocks[0].shape
    shape = jax.ShapeDtypeStruct((count, t * owners, d), blocks[0].dtype)
    return pl.pallas_call(
        functools.partial(join_kernel, owners, count),
        out_shape=shape,
        in_specs=[ANY] * owners,
        out_specs=ANY,
        scratch_shapes=[pltpu.SemaphoreType.DMA((owners,))],
        cost_estimate=cost(4 * math.prod(shape.shape)),
        compiler_params=SMALL,
        name="join",
    )(*blocks)


def attend_kernel(owners, capacity, first, count, skip, tiles, tiles_all, band, *refs):
    head_slot, mask, mid, before, after = refs[:5]
    q_blocks = refs[5 : 5 + owners]
    outs = refs[5 + owners : 5 + 2 * owners]
    lse_ref, q_all, kv_all, o_all, mask_all, head_of, used, sem_q, sem_kv, sem_m = refs[
        5 + 2 * owners :
    ]
    me = lax.axis_index("head")
    tile_base = lax.axis_index("slab") * tiles
    _, tok, dim = q_blocks[0].shape
    reach = (band - 1) // 2
    rows = tok * owners // tiles
    halo, own = reach * rows, tiles * rows
    scale = dim ** (-0.5)
    base2 = scale * math.log2(math.e)

    mask_copy = pltpu.make_async_copy(mask, mask_all, sem_m)
    mask_copy.start()
    copies = []
    for k in range(owners):
        start = lax.rem(me - k + owners, owners) * tok
        place = pl.ds(pl.multiple_of(start, tok), tok)
        copies.append(
            pltpu.make_async_copy(
                q_blocks[k].at[pl.ds(skip, count)], q_all.at[:, place], sem_q.at[k]
            )
        )
    for i, (source, start, size) in enumerate(
        ((before, 0, halo), (mid, halo, own), (after, halo + own, halo))
    ):
        copies.append(
            pltpu.make_async_copy(source, kv_all.at[:, pl.ds(start, size)], sem_kv.at[i])
        )
    for copy in copies:
        copy.start()

    invert(head_slot, head_of, used)
    mask_copy.wait()

    for copy in copies:
        copy.wait()
    for c in range(count):
        slot = me * capacity + first + c
        head = head_of[slot]
        valid = used[slot] > 0
        for t in range(tiles):
            queries = q_all[c, t * rows : (t + 1) * rows, :]
            keys = kv_all[c, t * rows : (t + band) * rows, :]
            values = kv_all[count + c, t * rows : (t + band) * rows, :]
            scores = lax.dot_general(
                queries, keys, (((1,), (1,)), ((), ())), preferred_element_type=jnp.float32
            )
            kept = []
            for b in range(band):
                tile = tile_base + t + b - reach
                flag = mask_all[b, t, head]
                allowed = (flag > 0) & (tile >= 0) & (tile < tiles_all)
                part = scores[:, b * rows : (b + 1) * rows]
                kept.append(jnp.where(allowed, part, -1e30))
            masked = jnp.concatenate(kept, axis=1)
            highest = jnp.max(masked, axis=1, keepdims=True)
            weights = jnp.exp2((masked - highest) * base2)
            total = jnp.sum(weights, axis=1, keepdims=True)
            summed = jnp.dot(
                weights.astype(jnp.bfloat16), values, preferred_element_type=jnp.float32
            )
            o_all[c, t * rows : (t + 1) * rows, :] = (summed / total).astype(jnp.bfloat16)
            lse = jnp.where(valid, highest * scale + jnp.log(total), 0.0)
            lse_ref[c : c + 1, t * rows : (t + 1) * rows] = jnp.transpose(
                jnp.broadcast_to(lse, (rows, 128))
            )[0:1, :]

    for k in range(owners):
        place = pl.ds(pl.multiple_of(lax.rem(me + k, owners) * tok, tok), tok)
        outs[k][...] = o_all[:, place, :]


def attend(head_slot, mask, near, q_blocks, capacity, first, count, skip, tiles, tiles_all, band):
    owners = len(q_blocks)
    _, tok, dim = q_blocks[0].shape
    rows = tok * owners // tiles
    out = jax.ShapeDtypeStruct((count, tok, dim), jnp.bfloat16)
    pairs = count * tok * owners * band * rows
    extended = tok * owners + (band - 1) * rows
    return pl.pallas_call(
        functools.partial(
            attend_kernel, owners, capacity, first, count, skip, tiles, tiles_all, band
        ),
        out_shape=[out] * owners + [jax.ShapeDtypeStruct((count, tok * owners), jnp.float32)],
        in_specs=[SMEM, HBM] + [ANY] * (owners + 3),
        out_specs=[VMEM] * (owners + 1),
        scratch_shapes=[
            pltpu.VMEM((count, tok * owners, dim), jnp.bfloat16),
            pltpu.VMEM((2 * count, extended, dim), jnp.bfloat16),
            pltpu.VMEM((count, tok * owners, dim), jnp.bfloat16),
            pltpu.SMEM(mask.shape, jnp.int32),
            pltpu.SMEM((owners * capacity,), jnp.int32),
            pltpu.SMEM((owners * capacity,), jnp.int32),
            pltpu.SemaphoreType.DMA((owners,)),
            pltpu.SemaphoreType.DMA((3,)),
            pltpu.SemaphoreType.DMA,
        ],
        cost_estimate=cost(
            4 * count * dim * (extended + tok * owners), 4 * pairs * dim, pairs
        ),
        compiler_params=LARGE,
        name="attend",
    )(head_slot, mask, *near, *q_blocks)


def unpack_kernel(owners, capacity, first, count, dim, head_slot, *refs):
    blocks = refs[:owners]
    out, head_of, used, sem = refs[-4:]
    me = lax.axis_index("head")
    invert(head_slot, head_of, used)

    def each(act):
        for k in range(owners):
            owner = lax.rem(me - k + owners, owners)
            for c in range(count):
                slot = owner * capacity + first + c
                columns = pl.ds(pl.multiple_of(head_of[slot] * dim, dim), dim)
                copy = pltpu.make_async_copy(
                    blocks[k].at[c], out.at[:, columns], sem.at[k * count + c]
                )
                pl.when(used[slot] > 0)(functools.partial(act, copy))

    each(lambda copy: copy.start())
    each(lambda copy: copy.wait())


def unpack(head_slot, blocks, target, capacity, first, shape):
    owners = len(blocks)
    count, tok, dim = blocks[0].shape
    operands = list(blocks) + ([] if target is None else [target])
    return pl.pallas_call(
        functools.partial(unpack_kernel, owners, capacity, first, count, dim),
        out_shape=shape,
        in_specs=[SMEM] + [ANY] * owners + ([] if target is None else [HBM]),
        out_specs=HBM,
        input_output_aliases={} if target is None else {owners + 1: 0},
        scratch_shapes=[
            pltpu.SMEM((owners * capacity,), jnp.int32),
            pltpu.SMEM((owners * capacity,), jnp.int32),
            pltpu.SemaphoreType.DMA((owners * count,)),
        ],
        cost_estimate=cost(4 * owners * count * tok * dim),
        compiler_params=SMALL,
        name="unpack",
    )(head_slot, *operands)


def exchange(blocks):
    owners = len(blocks)
    order = sorted(range(1, owners), key=lambda k: abs(2 * k - owners))
    moved = {
        k: lax.ppermute(blocks[k], "head", [(i, (i + k) % owners) for i in range(owners)])
        for k in order
    }
    return [blocks[0]] + [moved[k] for k in range(1, owners)]


def on_device(query_rows, key_rows, value_rows, tile_mask, head_slot):
    owners = lax.axis_size("head")
    slabs = lax.axis_size("slab")
    tok_dev, width = query_rows.shape
    heads, tiles, band = tile_mask.shape
    dim = width // heads
    capacity = (heads + owners - 1) // owners
    tok_slab = tok_dev * owners
    halo = (band - 1) // 2 * (tok_slab // tiles)
    mask = jnp.transpose(tile_mask, (2, 1, 0))
    half = (capacity + 1) // 2
    groups = [g for g in ((0, half), (half, capacity - half)) if g[1]]
    up = [(i, i + 1) for i in range(slabs - 1)]
    down = [(j, i) for i, j in up]

    stages, near, wait_for = [], [], ()
    for stage in range(len(groups) + 1):
        parts = []
        if stage < len(groups):
            parts += [(key_rows, *groups[stage]), (value_rows, *groups[stage])]
        if stage > 0:
            parts.append((query_rows, *groups[stage - 1]))
        waits = ()
        blocks = exchange(pack(head_slot, parts, owners, capacity, dim, waits))
        stages.append(blocks)
        if stage < len(groups):
            mid = join(blocks, 2 * groups[stage][1])
            last = lax.slice_in_dim(mid, tok_slab - halo, tok_slab, axis=1)
            lead = lax.slice_in_dim(mid, 0, halo, axis=1)
            before = lax.ppermute(last, "slab", up)
            after = lax.ppermute(lead, "slab", down)
            near.append((mid, before, after))

    target, lses = None, []
    for g, (first, count) in enumerate(groups):
        skip = 2 * groups[g + 1][1] if g + 1 < len(groups) else 0
        sizes = (capacity, first, count, skip, tiles, tiles * slabs, band)
        *outs, lse = attend(head_slot, mask, near[g], stages[g + 1], *sizes)
        lses.append(lse)
        shape = jax.ShapeDtypeStruct(query_rows.shape, query_rows.dtype)
        target = unpack(head_slot, exchange(outs), target, capacity, first, shape)
    return target, jnp.concatenate(lses, axis=0)


def solution(mesh):
    rows = P(("groups", "slab", "head"), None)
    in_specs = (rows, rows, rows, P(None, ("groups", "slab"), None), P())
    out_specs = (rows, P("head", ("groups", "slab")))
    return jax.shard_map(
        on_device, mesh=mesh, in_specs=in_specs, out_specs=out_specs, check_vma=False
    )
```

```python
import functools
import math

import jax
import jax.numpy as jnp
from jax import lax
from jax.experimental import pallas as pl
from jax.experimental.pallas import tpu as pltpu
from jax.sharding import PartitionSpec as P

HBM = pl.BlockSpec(memory_space=pltpu.HBM)
ANY = pl.BlockSpec(memory_space=pl.ANY)
SMEM = pl.BlockSpec(memory_space=pltpu.SMEM)
VMEM = pl.BlockSpec(memory_space=pltpu.VMEM)
SMALL = pltpu.CompilerParams(vmem_limit_bytes=4 * 1024 * 1024)
LARGE = pltpu.CompilerParams(vmem_limit_bytes=24 * 1024 * 1024)


SPLIT = 5
STAGES = ((('k', 0), ('v', 0)), (('k', 1), ('v', 1), ('q', 0)), (('q', 1),))
PACK_US = (0.0, 0.0, 0.0, 0.0)
JOIN_US = (0.0, 0.0)
QJOIN_US = (0.0, 0.0)
WAIT_LAST = False
ATTEND_US = (0.0, 0.0)
UNPACK_US = (0.0, 0.0)
CHAIN = True
HOLD = 0
ORDER = (2, 1, 3)


def hint(us):
    return pl.CostEstimate(flops=int(us * 1e9), bytes_accessed=int(us * 3e6), transcendentals=int(us * 1e6))


def in_hbm(x):
    return pltpu.with_memory_space_constraint(x, pltpu.HBM)


def invert(head_slot, head_of, used=None):
    for j in range(head_of.shape[0]):
        head_of[j] = 0
        if used is not None:
            used[j] = 0
    for h in range(head_slot.shape[0]):
        head_of[head_slot[h]] = h
        if used is not None:
            used[head_slot[h]] = 1


def pack_kernel(owners, capacity, dim, parts, sources, waited, head_slot, *refs):
    rows = refs[:sources]
    count_out = len(parts) * owners
    outs = refs[sources + waited : sources + waited + count_out]
    held = refs[sources + waited + count_out : 2 * sources + waited + count_out]
    slots, head_of, sem, sem_slots = refs[2 * sources + waited + count_out :]
    me = lax.axis_index("head")
    slot_copy = pltpu.make_async_copy(head_slot, slots, sem_slots)
    slot_copy.start()
    chunks = sem.shape[1]
    size = rows[0].shape[0] // chunks
    copies = []
    for i in range(sources):
        for j in range(chunks):
            place = pl.ds(j * size, size)
            copies.append(
                pltpu.make_async_copy(rows[i].at[place], held[i].at[place], sem.at[i, j])
            )
            copies[-1].start()
    slot_copy.wait()
    invert(slots, head_of)
    for copy in copies:
        copy.wait()
    for stage, part in enumerate(parts):
        for k in range(owners):
            owner = lax.rem(me + k, owners)
            place = 0
            for source, first, count in part:
                for c in range(count):
                    head = head_of[owner * capacity + first + c]
                    columns = pl.ds(pl.multiple_of(head * dim, dim), dim)
                    outs[stage * owners + k][place] = held[source][:, columns]
                    place += 1


def pack(head_slot, sources, stages, owners, capacity, dim, us, waits=()):
    names = sorted({name for held in stages for name, _, _ in held})
    rows = [sources[name] for name in names]
    tokens, dtype = rows[0].shape[0], rows[0].dtype
    shapes = []
    for held in stages:
        total = sum(count for _, _, count in held)
        shapes += [jax.ShapeDtypeStruct((total, tokens, dim), dtype)] * owners
    places = tuple(tuple((names.index(n), f, c) for n, f, c in held) for held in stages)
    chunks = max(tokens // 16, 1)
    packed = pl.pallas_call(
        functools.partial(pack_kernel, owners, capacity, dim, places, len(rows), len(waits)),
        out_shape=shapes,
        in_specs=[ANY] * (1 + len(rows) + len(waits)),
        out_specs=[VMEM] * len(shapes),
        scratch_shapes=[pltpu.VMEM(row.shape, row.dtype) for row in rows]
        + [
            pltpu.SMEM(head_slot.shape, jnp.int32),
            pltpu.SMEM((owners * capacity,), jnp.int32),
            pltpu.SemaphoreType.DMA((len(rows), chunks)),
            pltpu.SemaphoreType.DMA,
        ],
        cost_estimate=hint(us),
        compiler_params=SMALL,
        name="pack",
    )(*[in_hbm(x) for x in (head_slot, *rows)], *waits)
    return [packed[i * owners : (i + 1) * owners] for i in range(len(stages))]


def join_kernel(owners, skip, count, *refs):
    blocks, out, sem = refs[:owners], refs[owners], refs[owners + 1]
    me = lax.axis_index("head")
    tokens = blocks[0].shape[1]
    copies = []
    for k in range(owners):
        start = lax.rem(me - k + owners, owners) * tokens
        place = pl.ds(pl.multiple_of(start, tokens), tokens)
        copies.append(
            pltpu.make_async_copy(blocks[k].at[pl.ds(skip, count)], out.at[:, place], sem.at[k])
        )
        copies[-1].start()
    for copy in copies:
        copy.wait()


def join(blocks, skip, count, us):
    owners = len(blocks)
    _, t, d = blocks[0].shape
    shape = jax.ShapeDtypeStruct((count, t * owners, d), blocks[0].dtype)
    return pl.pallas_call(
        functools.partial(join_kernel, owners, skip, count),
        out_shape=shape,
        in_specs=[ANY] * owners,
        out_specs=ANY,
        scratch_shapes=[pltpu.SemaphoreType.DMA((owners,))],
        cost_estimate=hint(us),
        compiler_params=SMALL,
        name="join",
    )(*blocks)


def attend_kernel(owners, capacity, first, count, tiles, tiles_all, band, *refs):
    head_slot, mask, mid, even, odd, q_all = refs[:6]
    outs = refs[6 : 6 + owners]
    lse_ref, kv_all, o_all, logits, weights, totals = refs[6 + owners : 12 + owners]
    mask_all, slots, head_of, used, sem_kv, sem_m = refs[12 + owners :]
    me = lax.axis_index("head")
    tile_base = lax.axis_index("slab") * tiles
    _, tok_slab, dim = q_all.shape
    tok = tok_slab // owners
    reach = (band - 1) // 2
    rows = tok_slab // tiles
    halo, own = reach * rows, tiles * rows
    scale = dim ** (-0.5)
    base2 = scale * math.log2(math.e)
    spans = logits.shape[1]
    span = tiles // spans

    small = [
        pltpu.make_async_copy(mask, mask_all, sem_m.at[0]),
        pltpu.make_async_copy(head_slot, slots, sem_m.at[1]),
    ]
    lower = lax.rem(lax.axis_index("slab"), 2) == 0
    places = (
        (mid, halo, own),
        (even, pl.multiple_of(jnp.where(lower, halo + own, 0), rows), halo),
        (odd, pl.multiple_of(jnp.where(lower, 0, halo + own), rows), halo),
    )
    large = [
        pltpu.make_async_copy(source, kv_all.at[:, pl.ds(start, size)], sem_kv.at[i])
        for i, (source, start, size) in enumerate(places)
    ]
    for copy in large + small:
        copy.start()
    for copy in large:
        copy.wait()

    for c in range(count):
        for u in range(spans):
            low = u * span * rows
            logits[c, u] = lax.dot_general(
                kv_all[c, low : low + (span - 1 + band) * rows, :],
                q_all[c, low : low + span * rows, :],
                (((1,), (1,)), ((), ())),
                preferred_element_type=jnp.float32,
            )

    for copy in small:
        copy.wait()
    invert(slots, head_of, used)

    for c in range(count):
        slot = me * capacity + first + c
        head = head_of[slot]
        valid = used[slot] > 0
        for t in range(tiles):
            u, w = t // span, t % span
            columns = slice(w * rows, (w + 1) * rows)
            allowed, highest = [], None
            for b in range(band):
                tile = tile_base + t + b - reach
                flag = mask_all[b, t, head]
                allowed.append((flag > 0) & (tile >= 0) & (tile < tiles_all))
                part = logits[c, u, (w + b) * rows : (w + b + 1) * rows, columns]
                part = jnp.max(part.reshape(rows // 8, 8, rows), axis=0)
                part = jnp.where(allowed[b], part, -1e30)
                highest = part if highest is None else jnp.maximum(highest, part)
            highest = jnp.max(highest, axis=0, keepdims=True)
            total = None
            for b in range(band):
                shift = jnp.where(allowed[b], highest * base2, 1e30)
                part = logits[c, u, (w + b) * rows : (w + b + 1) * rows, columns]
                part = jnp.exp2(part * base2 - shift)
                weights[c * tiles + t, b * rows : (b + 1) * rows, :] = part.astype(jnp.bfloat16)
                part = jnp.sum(part.reshape(rows // 8, 8, rows), axis=0)
                total = part if total is None else total + part
            total = jnp.sum(total, axis=0, keepdims=True)
            place = slice(t * rows, (t + 1) * rows)
            totals[c : c + 1, place] = total
            lse = highest * scale + jnp.log(total)
            lse_ref[c : c + 1, place] = jnp.where(valid, lse, 0.0)

    for c in range(count):
        for t in range(tiles):
            place = slice(t * rows, (t + 1) * rows)
            summed = lax.dot_general(
                kv_all[count + c, t * rows : (t + band) * rows, :],
                weights[c * tiles + t],
                (((0,), (0,)), ((), ())),
                preferred_element_type=jnp.float32,
            )
            o_all[c, place, :] = jnp.transpose(summed / totals[c : c + 1, place]).astype(
                jnp.bfloat16
            )

    for k in range(owners):
        place = pl.ds(pl.multiple_of(lax.rem(me + k, owners) * tok, tok), tok)
        outs[k][...] = o_all[:, place, :]


def attend(head_slot, mask, near, queries, us, owners, *sizes):
    capacity, first, count, tiles, tiles_all, band = sizes
    _, tok_slab, dim = queries.shape
    rows = tok_slab // tiles
    span = 2 if tiles % 2 == 0 else 1
    out = jax.ShapeDtypeStruct((count, tok_slab // owners, dim), jnp.bfloat16)
    extended = tok_slab + (band - 1) * rows
    slots = owners * capacity
    return pl.pallas_call(
        functools.partial(attend_kernel, owners, capacity, first, count, tiles, tiles_all, band),
        out_shape=[out] * owners + [jax.ShapeDtypeStruct((count, tok_slab), jnp.float32)],
        in_specs=[ANY] * 5 + [VMEM],
        out_specs=[VMEM] * (owners + 1),
        scratch_shapes=[
            pltpu.VMEM((2 * count, extended, dim), jnp.bfloat16),
            pltpu.VMEM((count, tok_slab, dim), jnp.bfloat16),
            pltpu.VMEM((count, tiles // span, (span - 1 + band) * rows, span * rows), jnp.float32),
            pltpu.VMEM((count * tiles, band * rows, rows), jnp.bfloat16),
            pltpu.VMEM((count, tok_slab), jnp.float32),
            pltpu.SMEM(mask.shape, jnp.int32),
            pltpu.SMEM(head_slot.shape, jnp.int32),
            pltpu.SMEM((slots,), jnp.int32),
            pltpu.SMEM((slots,), jnp.int32),
            pltpu.SemaphoreType.DMA((3,)),
            pltpu.SemaphoreType.DMA((2,)),
        ],
        cost_estimate=hint(us),
        compiler_params=LARGE,
        name="attend",
    )(in_hbm(head_slot), in_hbm(mask), *near, queries)


def unpack_kernel(owners, capacity, first, count, dim, head_slot, *refs):
    blocks = refs[:owners]
    out, slots, head_of, used, sem, sem_slots = refs[-6:]
    me = lax.axis_index("head")
    slot_copy = pltpu.make_async_copy(head_slot, slots, sem_slots)
    slot_copy.start()
    slot_copy.wait()
    invert(slots, head_of, used)

    def each(act):
        for k in range(owners):
            owner = lax.rem(me - k + owners, owners)
            for c in range(count):
                slot = owner * capacity + first + c
                columns = pl.ds(pl.multiple_of(head_of[slot] * dim, dim), dim)
                copy = pltpu.make_async_copy(
                    blocks[k].at[c], out.at[:, columns], sem.at[k * count + c]
                )
                if owners * capacity == head_slot.shape[0]:
                    act(copy)
                else:
                    pl.when(used[slot] > 0)(functools.partial(act, copy))

    each(lambda copy: copy.start())
    each(lambda copy: copy.wait())


def unpack(head_slot, blocks, target, capacity, first, shape, us):
    owners = len(blocks)
    count, tok, dim = blocks[0].shape
    operands = list(blocks) + ([] if target is None else [target])
    return pl.pallas_call(
        functools.partial(unpack_kernel, owners, capacity, first, count, dim),
        out_shape=shape,
        in_specs=[ANY] * (owners + 1) + ([] if target is None else [HBM]),
        out_specs=HBM,
        input_output_aliases={} if target is None else {owners + 1: 0},
        scratch_shapes=[
            pltpu.SMEM(head_slot.shape, jnp.int32),
            pltpu.SMEM((owners * capacity,), jnp.int32),
            pltpu.SMEM((owners * capacity,), jnp.int32),
            pltpu.SemaphoreType.DMA((owners * count,)),
            pltpu.SemaphoreType.DMA,
        ],
        cost_estimate=hint(us),
        compiler_params=SMALL,
        name="unpack",
    )(in_hbm(head_slot), *operands)


def exchange(blocks):
    owners = len(blocks)
    order = ORDER if len(ORDER) == owners - 1 else range(1, owners)
    moved = {
        k: lax.ppermute(blocks[k], "head", [(i, (i + k) % owners) for i in range(owners)])
        for k in order
    }
    return [blocks[0]] + [moved[k] for k in range(1, owners)]


def swap(mid, parity, halo):
    slabs, length = lax.axis_size("slab"), mid.shape[1]
    pairs = [(i, i + 1) for i in range(parity, slabs - 1, 2)]
    if halo < length:
        lower = lax.rem(lax.axis_index("slab"), 2) == parity
        start = jnp.where(lower, length - halo, 0)
        mid = lax.dynamic_slice_in_dim(mid, start, halo, 1)
    return lax.ppermute(mid, "slab", pairs + [(j, i) for i, j in pairs])


def after(x, done):
    return pl.pallas_call(
        lambda *refs: None,
        out_shape=jax.ShapeDtypeStruct(x.shape, x.dtype),
        in_specs=[ANY, ANY],
        out_specs=ANY,
        input_output_aliases={0: 0},
        cost_estimate=hint(0.0),
        compiler_params=SMALL,
        name="after",
    )(x, done)


def on_device(query_rows, key_rows, value_rows, tile_mask, head_slot):
    owners = lax.axis_size("head")
    slabs = lax.axis_size("slab")
    tok_dev, width = query_rows.shape
    heads, tiles, band = tile_mask.shape
    dim = width // heads
    capacity = (heads + owners - 1) // owners
    tok_slab = tok_dev * owners
    halo = (band - 1) // 2 * (tok_slab // tiles)
    mask = jnp.transpose(tile_mask, (2, 1, 0))
    half = (SPLIT * capacity + 9) // 10
    groups = ((0, half), (half, capacity - half))
    source = {"q": query_rows, "k": key_rows, "v": value_rows}

    sizes = [[(name, *groups[g]) for name, g in held] for held in STAGES]
    args = (owners, capacity, dim)
    packed = pack(head_slot, source, sizes[:1], *args, PACK_US[0])
    if len(sizes) > 1:
        packed += pack(head_slot, source, sizes[1:], *args, PACK_US[1], packed[0][:1] if CHAIN else ())
    moved = [exchange(blocks) for blocks in packed]
    near, queries = {}, {}
    for blocks, held in zip(moved, STAGES):
        skip = 0
        for name, g in held:
            count = groups[g][1]
            if name == "q":
                queries[g] = join(blocks, skip, count, QJOIN_US[g])
            if name == "k":
                mid = join(blocks, skip, 2 * count, JOIN_US[g])
                if g == 1 and HOLD:
                    mid = after(mid, moved[-1][HOLD])
                even = swap(mid, 0, halo)
                mid = after(mid, even)
                near[g] = (mid, even, swap(mid, 1, halo))
            skip += count

    target, lses = None, []
    for g, (first, count) in enumerate(groups):
        sizes = (owners, capacity, first, count, tiles, tiles * slabs, band)
        *outs, lse = attend(head_slot, mask, near[g], queries[g], ATTEND_US[g], *sizes)
        lses.append(lse)
        shape = jax.ShapeDtypeStruct(query_rows.shape, query_rows.dtype)
        target = unpack(head_slot, exchange(outs), target, capacity, first, shape, UNPACK_US[g])
    return target, jnp.concatenate(lses, axis=0)


def solution(mesh):
    rows = P(("groups", "slab", "head"), None)
    in_specs = (rows, rows, rows, P(None, ("groups", "slab"), None), P())
    out_specs = (rows, P("head", ("groups", "slab")))
    return jax.shard_map(
        on_device, mesh=mesh, in_specs=in_specs, out_specs=out_specs, check_vma=False
    )
```

```python
import functools
import math

import jax
import jax.numpy as jnp
from jax import lax
from jax.experimental import pallas as pl
from jax.experimental.pallas import tpu as pltpu
from jax.sharding import PartitionSpec as P

HBM = pl.BlockSpec(memory_space=pltpu.HBM)
ANY = pl.BlockSpec(memory_space=pl.ANY)
SMEM = pl.BlockSpec(memory_space=pltpu.SMEM)
VMEM = pl.BlockSpec(memory_space=pltpu.VMEM)
SMALL = pltpu.CompilerParams(vmem_limit_bytes=4 * 1024 * 1024)
LARGE = pltpu.CompilerParams(vmem_limit_bytes=24 * 1024 * 1024)


SPLIT = 5
STAGES = ((('k', 0), ('v', 0)), (('k', 1), ('v', 1), ('q', 0)), (('q', 1),))
PACK_US = (0.0, 0.0, 0.0, 0.0)
JOIN_US = (0.0, 0.0)
QJOIN_US = (0.0, 0.0)
ATTEND_US = (0.0, 0.0)
UNPACK_US = (0.0, 0.0)
FIRST = (1, 0)
ORDER = (1, 3, 2)


def hint(us):
    return pl.CostEstimate(flops=int(us * 1e9), bytes_accessed=int(us * 3e6), transcendentals=int(us * 1e6))


def in_hbm(x):
    return pltpu.with_memory_space_constraint(x, pltpu.HBM)


def invert(head_slot, head_of, used=None):
    if head_of.shape[0] > head_slot.shape[0] or used is not None:
        for j in range(head_of.shape[0]):
            head_of[j] = 0
            if used is not None:
                used[j] = 0
    for h in range(head_slot.shape[0]):
        head_of[head_slot[h]] = h
        if used is not None:
            used[head_slot[h]] = 1


def pack_kernel(owners, capacity, dim, parts, sources, waited, head_slot, *refs):
    rows = refs[:sources]
    count_out = len(parts) * owners
    outs = refs[sources + waited : sources + waited + count_out]
    held = refs[sources + waited + count_out : 2 * sources + waited + count_out]
    slots, head_of, sem, sem_slots = refs[2 * sources + waited + count_out :]
    me = lax.axis_index("head")
    slot_copy = pltpu.make_async_copy(head_slot, slots, sem_slots)
    slot_copy.start()
    chunks = sem.shape[1]
    size = rows[0].shape[0] // chunks
    copies = []
    for i in range(sources):
        for j in range(chunks):
            place = pl.ds(j * size, size)
            copies.append(
                pltpu.make_async_copy(rows[i].at[place], held[i].at[place], sem.at[i, j])
            )
            copies[-1].start()
    slot_copy.wait()
    invert(slots, head_of)
    for copy in copies:
        copy.wait()
    for stage, part in enumerate(parts):
        for k in range(owners):
            owner = lax.rem(me + k, owners)
            place = 0
            for source, first, count in part:
                for c in range(count):
                    head = head_of[owner * capacity + first + c]
                    columns = pl.ds(pl.multiple_of(head * dim, dim), dim)
                    outs[stage * owners + k][place] = held[source][:, columns]
                    place += 1


def pack(head_slot, sources, stages, owners, capacity, dim, us, waits=()):
    names = sorted({name for held in stages for name, _, _ in held})
    rows = [sources[name] for name in names]
    tokens, dtype = rows[0].shape[0], rows[0].dtype
    shapes = []
    for held in stages:
        total = sum(count for _, _, count in held)
        shapes += [jax.ShapeDtypeStruct((total, tokens, dim), dtype)] * owners
    places = tuple(tuple((names.index(n), f, c) for n, f, c in held) for held in stages)
    chunks = max(tokens // 16, 1)
    packed = pl.pallas_call(
        functools.partial(pack_kernel, owners, capacity, dim, places, len(rows), len(waits)),
        out_shape=shapes,
        in_specs=[ANY] * (1 + len(rows) + len(waits)),
        out_specs=[VMEM] * len(shapes),
        scratch_shapes=[pltpu.VMEM(row.shape, row.dtype) for row in rows]
        + [
            pltpu.SMEM(head_slot.shape, jnp.int32),
            pltpu.SMEM((owners * capacity,), jnp.int32),
            pltpu.SemaphoreType.DMA((len(rows), chunks)),
            pltpu.SemaphoreType.DMA,
        ],
        cost_estimate=hint(us),
        compiler_params=SMALL,
        name="pack",
    )(*[in_hbm(x) for x in (head_slot, *rows)], *waits)
    return [packed[i * owners : (i + 1) * owners] for i in range(len(stages))]


def join_kernel(owners, skip, count, *refs):
    blocks, out, sem = refs[:owners], refs[owners], refs[owners + 1]
    me = lax.axis_index("head")
    tokens = blocks[0].shape[1]
    copies = []
    for k in range(owners):
        start = lax.rem(me - k + owners, owners) * tokens
        place = pl.ds(pl.multiple_of(start, tokens), tokens)
        copies.append(
            pltpu.make_async_copy(blocks[k].at[pl.ds(skip, count)], out.at[:, place], sem.at[k])
        )
        copies[-1].start()
    for copy in copies:
        copy.wait()


def join(blocks, skip, count, us):
    owners = len(blocks)
    _, t, d = blocks[0].shape
    shape = jax.ShapeDtypeStruct((count, t * owners, d), blocks[0].dtype)
    return pl.pallas_call(
        functools.partial(join_kernel, owners, skip, count),
        out_shape=shape,
        in_specs=[ANY] * owners,
        out_specs=ANY,
        scratch_shapes=[pltpu.SemaphoreType.DMA((owners,))],
        cost_estimate=hint(us),
        compiler_params=SMALL,
        name="join",
    )(*blocks)


def attend_kernel(owners, capacity, first, count, tiles, tiles_all, band, *refs):
    head_slot, mask, mid, even, odd, q_all = refs[:6]
    outs = refs[6 : 6 + owners]
    lse_ref, kv_all, o_all, logits, weights, totals = refs[6 + owners : 12 + owners]
    mask_all, slots, head_of, used, sem_kv, sem_m = refs[12 + owners :]
    me = lax.axis_index("head")
    tile_base = lax.axis_index("slab") * tiles
    _, tok_slab, dim = q_all.shape
    tok = tok_slab // owners
    reach = (band - 1) // 2
    rows = tok_slab // tiles
    halo, own = reach * rows, tiles * rows
    scale = dim ** (-0.5)
    base2 = scale * math.log2(math.e)
    spans = logits.shape[1]
    span = tiles // spans

    small = [
        pltpu.make_async_copy(mask, mask_all, sem_m.at[0]),
        pltpu.make_async_copy(head_slot, slots, sem_m.at[1]),
    ]
    lower = lax.rem(lax.axis_index("slab"), 2) == 0
    places = (
        (mid, halo, own),
        (even, pl.multiple_of(jnp.where(lower, halo + own, 0), rows), halo),
        (odd, pl.multiple_of(jnp.where(lower, 0, halo + own), rows), halo),
    )
    large = [
        pltpu.make_async_copy(source, kv_all.at[:, pl.ds(start, size)], sem_kv.at[i])
        for i, (source, start, size) in enumerate(places)
    ]
    for copy in large + small:
        copy.start()
    for copy in large:
        copy.wait()

    for c in range(count):
        for u in range(spans):
            low = u * span * rows
            logits[c, u] = lax.dot_general(
                kv_all[c, low : low + (span - 1 + band) * rows, :],
                q_all[c, low : low + span * rows, :],
                (((1,), (1,)), ((), ())),
                preferred_element_type=jnp.float32,
            )

    for copy in small:
        copy.wait()
    invert(slots, head_of, used)

    for c in range(count):
        slot = me * capacity + first + c
        head = head_of[slot]
        valid = used[slot] > 0
        for t in range(tiles):
            u, w = t // span, t % span
            columns = slice(w * rows, (w + 1) * rows)
            allowed, highest = [], None
            for b in range(band):
                tile = tile_base + t + b - reach
                flag = mask_all[b, t, head]
                allowed.append((flag > 0) & (tile >= 0) & (tile < tiles_all))
                part = logits[c, u, (w + b) * rows : (w + b + 1) * rows, columns]
                part = jnp.max(part.reshape(rows // 8, 8, rows), axis=0)
                part = jnp.where(allowed[b], part, -1e30)
                highest = part if highest is None else jnp.maximum(highest, part)
            highest = jnp.max(highest, axis=0, keepdims=True)
            total = None
            for b in range(band):
                shift = jnp.where(allowed[b], highest * base2, 1e30)
                part = logits[c, u, (w + b) * rows : (w + b + 1) * rows, columns]
                part = jnp.exp2(part * base2 - shift)
                weights[c * tiles + t, b * rows : (b + 1) * rows, :] = part.astype(jnp.bfloat16)
                part = jnp.sum(part.reshape(rows // 8, 8, rows), axis=0)
                total = part if total is None else total + part
            total = jnp.sum(total, axis=0, keepdims=True)
            place = slice(t * rows, (t + 1) * rows)
            totals[c : c + 1, place] = total
            lse = highest * scale + jnp.log(total)
            lse_ref[c : c + 1, place] = jnp.where(valid, lse, 0.0)

    for c in range(count):
        for t in range(tiles):
            place = slice(t * rows, (t + 1) * rows)
            summed = lax.dot_general(
                kv_all[count + c, t * rows : (t + band) * rows, :],
                weights[c * tiles + t],
                (((0,), (0,)), ((), ())),
                preferred_element_type=jnp.float32,
            )
            o_all[c, place, :] = jnp.transpose(summed / totals[c : c + 1, place]).astype(
                jnp.bfloat16
            )

    for k in range(owners):
        place = pl.ds(pl.multiple_of(lax.rem(me + k, owners) * tok, tok), tok)
        outs[k][...] = o_all[:, place, :]


def attend(head_slot, mask, near, queries, us, owners, *sizes):
    capacity, first, count, tiles, tiles_all, band = sizes
    _, tok_slab, dim = queries.shape
    rows = tok_slab // tiles
    span = 2 if tiles % 2 == 0 else 1
    out = jax.ShapeDtypeStruct((count, tok_slab // owners, dim), jnp.bfloat16)
    extended = tok_slab + (band - 1) * rows
    slots = owners * capacity
    return pl.pallas_call(
        functools.partial(attend_kernel, owners, capacity, first, count, tiles, tiles_all, band),
        out_shape=[out] * owners + [jax.ShapeDtypeStruct((count, tok_slab), jnp.float32)],
        in_specs=[ANY] * 5 + [VMEM],
        out_specs=[VMEM] * (owners + 1),
        scratch_shapes=[
            pltpu.VMEM((2 * count, extended, dim), jnp.bfloat16),
            pltpu.VMEM((count, tok_slab, dim), jnp.bfloat16),
            pltpu.VMEM((count, tiles // span, (span - 1 + band) * rows, span * rows), jnp.float32),
            pltpu.VMEM((count * tiles, band * rows, rows), jnp.bfloat16),
            pltpu.VMEM((count, tok_slab), jnp.float32),
            pltpu.SMEM(mask.shape, jnp.int32),
            pltpu.SMEM(head_slot.shape, jnp.int32),
            pltpu.SMEM((slots,), jnp.int32),
            pltpu.SMEM((slots,), jnp.int32),
            pltpu.SemaphoreType.DMA((3,)),
            pltpu.SemaphoreType.DMA((2,)),
        ],
        cost_estimate=hint(us),
        compiler_params=LARGE,
        name="attend",
    )(in_hbm(head_slot), in_hbm(mask), *near, queries)


def unpack_kernel(owners, capacity, first, count, dim, head_slot, *refs):
    blocks = refs[:owners]
    out, head_of, used, sem = refs[-4:]
    me = lax.axis_index("head")
    whole = owners * capacity == head_slot.shape[0]
    invert(head_slot, head_of, None if whole else used)

    def each(act):
        for k in range(owners):
            owner = lax.rem(me - k + owners, owners)
            for c in range(count):
                slot = owner * capacity + first + c
                columns = pl.ds(pl.multiple_of(head_of[slot] * dim, dim), dim)
                copy = pltpu.make_async_copy(
                    blocks[k].at[c], out.at[:, columns], sem.at[k * count + c]
                )
                if whole:
                    act(copy)
                else:
                    pl.when(used[slot] > 0)(functools.partial(act, copy))

    each(lambda copy: copy.start())
    each(lambda copy: copy.wait())


def unpack(head_slot, blocks, target, capacity, first, shape, us):
    owners = len(blocks)
    count, tok, dim = blocks[0].shape
    operands = list(blocks) + ([] if target is None else [target])
    return pl.pallas_call(
        functools.partial(unpack_kernel, owners, capacity, first, count, dim),
        out_shape=shape,
        in_specs=[SMEM] + [ANY] * owners + ([] if target is None else [HBM]),
        out_specs=HBM,
        input_output_aliases={} if target is None else {owners + 1: 0},
        scratch_shapes=[
            pltpu.SMEM((owners * capacity,), jnp.int32),
            pltpu.SMEM((owners * capacity,), jnp.int32),
            pltpu.SemaphoreType.DMA((owners * count,)),
        ],
        cost_estimate=hint(us),
        compiler_params=SMALL,
        name="unpack",
    )(head_slot, *operands)


def exchange(blocks):
    owners = len(blocks)
    order = ORDER if len(ORDER) == owners - 1 else range(1, owners)
    moved = {
        k: lax.ppermute(blocks[k], "head", [(i, (i + k) % owners) for i in range(owners)])
        for k in order
    }
    return [blocks[0]] + [moved[k] for k in range(1, owners)]


def swap(mid, parity, halo):
    slabs, length = lax.axis_size("slab"), mid.shape[1]
    pairs = [(i, i + 1) for i in range(parity, slabs - 1, 2)]
    if halo < length:
        lower = lax.rem(lax.axis_index("slab"), 2) == parity
        start = jnp.where(lower, length - halo, 0)
        mid = lax.dynamic_slice_in_dim(mid, start, halo, 1)
    return lax.ppermute(mid, "slab", pairs + [(j, i) for i, j in pairs])


def after(x, done):
    return pl.pallas_call(
        lambda *refs: None,
        out_shape=jax.ShapeDtypeStruct(x.shape, x.dtype),
        in_specs=[ANY, ANY],
        out_specs=ANY,
        input_output_aliases={0: 0},
        cost_estimate=hint(0.0),
        compiler_params=SMALL,
        name="after",
    )(x, done)


def on_device(query_rows, key_rows, value_rows, tile_mask, head_slot):
    owners = lax.axis_size("head")
    slabs = lax.axis_size("slab")
    tok_dev, width = query_rows.shape
    heads, tiles, band = tile_mask.shape
    dim = width // heads
    capacity = (heads + owners - 1) // owners
    tok_slab = tok_dev * owners
    halo = (band - 1) // 2 * (tok_slab // tiles)
    mask = jnp.transpose(tile_mask, (2, 1, 0))
    half = (SPLIT * capacity + 9) // 10
    groups = ((0, half), (half, capacity - half))
    source = {"q": query_rows, "k": key_rows, "v": value_rows}

    sizes = [[(name, *groups[g]) for name, g in held] for held in STAGES]
    args = (owners, capacity, dim)
    packed = pack(head_slot, source, sizes[:1], *args, PACK_US[0])
    if len(sizes) > 1:
        packed += pack(head_slot, source, sizes[1:], *args, PACK_US[1], packed[0][:1])
    moved = [exchange(blocks) for blocks in packed]
    near, queries = {}, {}
    for blocks, held in zip(moved, STAGES):
        skip = 0
        for name, g in held:
            count = groups[g][1]
            if name == "q":
                queries[g] = join(blocks, skip, count, QJOIN_US[g])
            if name == "k":
                mid = join(blocks, skip, 2 * count, JOIN_US[g])
                lead = FIRST[g]
                one = swap(mid, lead, halo)
                mid = after(mid, one)
                two = swap(mid, 1 - lead, halo)
                near[g] = (mid, two, one) if lead else (mid, one, two)
            skip += count

    target, lses = None, []
    for g, (first, count) in enumerate(groups):
        sizes = (owners, capacity, first, count, tiles, tiles * slabs, band)
        *outs, lse = attend(head_slot, mask, near[g], queries[g], ATTEND_US[g], *sizes)
        lses.append(lse)
        shape = jax.ShapeDtypeStruct(query_rows.shape, query_rows.dtype)
        target = unpack(head_slot, exchange(outs), target, capacity, first, shape, UNPACK_US[g])
    return target, jnp.concatenate(lses, axis=0)


def solution(mesh):
    rows = P(("groups", "slab", "head"), None)
    in_specs = (rows, rows, rows, P(None, ("groups", "slab"), None), P())
    out_specs = (rows, P("head", ("groups", "slab")))
    return jax.shard_map(
        on_device, mesh=mesh, in_specs=in_specs, out_specs=out_specs, check_vma=False
    )
```

```python
import functools
import math

import jax
import jax.numpy as jnp
from jax import lax
from jax.experimental import pallas as pl
from jax.experimental.pallas import tpu as pltpu
from jax.sharding import PartitionSpec as P

HBM = pl.BlockSpec(memory_space=pltpu.HBM)
ANY = pl.BlockSpec(memory_space=pl.ANY)
SMEM = pl.BlockSpec(memory_space=pltpu.SMEM)
VMEM = pl.BlockSpec(memory_space=pltpu.VMEM)
SMALL = pltpu.CompilerParams(vmem_limit_bytes=4 * 1024 * 1024)
LARGE = pltpu.CompilerParams(vmem_limit_bytes=24 * 1024 * 1024)


SPLIT = 5
STAGES = ((('k', 0), ('v', 0)), (('k', 1), ('v', 1), ('q', 0)), (('q', 1),))
PACK_US = (0.0, 0.0, 0.0, 0.0)
JOIN_US = (0.0, 0.0)
QJOIN_US = (0.0, 0.0)
ATTEND_US = (0.0, 0.0)
UNPACK_US = (0.0, 0.0)
FIRST = (1, 0)
ORDER = (1, 3, 2)


def hint(us):
    return pl.CostEstimate(flops=int(us * 1e9), bytes_accessed=int(us * 3e6), transcendentals=int(us * 1e6))


def in_hbm(x):
    return pltpu.with_memory_space_constraint(x, pltpu.HBM)


def invert(head_slot, head_of, used=None):
    if head_of.shape[0] > head_slot.shape[0] or used is not None:
        for j in range(head_of.shape[0]):
            head_of[j] = 0
            if used is not None:
                used[j] = 0
    for h in range(head_slot.shape[0]):
        head_of[head_slot[h]] = h
        if used is not None:
            used[head_slot[h]] = 1


def pack_kernel(owners, capacity, dim, parts, sources, waited, head_slot, *refs):
    rows = refs[:sources]
    count_out = len(parts) * owners
    outs = refs[sources + waited : sources + waited + count_out]
    held = refs[sources + waited + count_out : 2 * sources + waited + count_out]
    slots, head_of, sem, sem_slots = refs[2 * sources + waited + count_out :]
    me = lax.axis_index("head")
    slot_copy = pltpu.make_async_copy(head_slot, slots, sem_slots)
    slot_copy.start()
    chunks = sem.shape[1]
    size = rows[0].shape[0] // chunks
    copies = []
    for j in range(chunks):
        for i in range(sources):
            place = pl.ds(j * size, size)
            copies.append(
                pltpu.make_async_copy(rows[i].at[place], held[i].at[place], sem.at[i, j])
            )
            copies[-1].start()
    slot_copy.wait()
    invert(slots, head_of)
    for j in range(chunks):
        for i in range(sources):
            copies[j * sources + i].wait()
        place = slice(j * size, (j + 1) * size)
        for stage, part in enumerate(parts):
            for k in range(owners):
                owner = lax.rem(me + k, owners)
                at = 0
                for source, first, count in part:
                    for c in range(count):
                        head = head_of[owner * capacity + first + c]
                        columns = pl.ds(pl.multiple_of(head * dim, dim), dim)
                        outs[stage * owners + k][at, place, :] = held[source][place, columns]
                        at += 1


def pack(head_slot, sources, stages, owners, capacity, dim, us, waits=()):
    names = sorted({name for held in stages for name, _, _ in held})
    rows = [sources[name] for name in names]
    tokens, dtype = rows[0].shape[0], rows[0].dtype
    shapes = []
    for held in stages:
        total = sum(count for _, _, count in held)
        shapes += [jax.ShapeDtypeStruct((total, tokens, dim), dtype)] * owners
    places = tuple(tuple((names.index(n), f, c) for n, f, c in held) for held in stages)
    chunks = max(tokens // 16, 1)
    packed = pl.pallas_call(
        functools.partial(pack_kernel, owners, capacity, dim, places, len(rows), len(waits)),
        out_shape=shapes,
        in_specs=[ANY] * (1 + len(rows) + len(waits)),
        out_specs=[VMEM] * len(shapes),
        scratch_shapes=[pltpu.VMEM(row.shape, row.dtype) for row in rows]
        + [
            pltpu.SMEM(head_slot.shape, jnp.int32),
            pltpu.SMEM((owners * capacity,), jnp.int32),
            pltpu.SemaphoreType.DMA((len(rows), chunks)),
            pltpu.SemaphoreType.DMA,
        ],
        cost_estimate=hint(us),
        compiler_params=SMALL,
        name="pack",
    )(*[in_hbm(x) for x in (head_slot, *rows)], *waits)
    return [packed[i * owners : (i + 1) * owners] for i in range(len(stages))]


def join_kernel(owners, skip, count, *refs):
    blocks, out, sem = refs[:owners], refs[owners], refs[owners + 1]
    me = lax.axis_index("head")
    tokens = blocks[0].shape[1]
    copies = []
    for k in range(owners):
        start = lax.rem(me - k + owners, owners) * tokens
        place = pl.ds(pl.multiple_of(start, tokens), tokens)
        copies.append(
            pltpu.make_async_copy(blocks[k].at[pl.ds(skip, count)], out.at[:, place], sem.at[k])
        )
        copies[-1].start()
    for copy in copies:
        copy.wait()


def join(blocks, skip, count, us):
    owners = len(blocks)
    _, t, d = blocks[0].shape
    shape = jax.ShapeDtypeStruct((count, t * owners, d), blocks[0].dtype)
    return pl.pallas_call(
        functools.partial(join_kernel, owners, skip, count),
        out_shape=shape,
        in_specs=[ANY] * owners,
        out_specs=ANY,
        scratch_shapes=[pltpu.SemaphoreType.DMA((owners,))],
        cost_estimate=hint(us),
        compiler_params=SMALL,
        name="join",
    )(*blocks)


def attend_kernel(owners, capacity, first, count, tiles, tiles_all, band, *refs):
    head_slot, mask, mid, even, odd, q_all = refs[:6]
    outs = refs[6 : 6 + owners]
    lse_ref, kv_all, o_all, logits, weights, totals = refs[6 + owners : 12 + owners]
    mask_all, slots, head_of, used, sem_kv, sem_m = refs[12 + owners :]
    me = lax.axis_index("head")
    tile_base = lax.axis_index("slab") * tiles
    _, tok_slab, dim = q_all.shape
    tok = tok_slab // owners
    reach = (band - 1) // 2
    rows = tok_slab // tiles
    halo, own = reach * rows, tiles * rows
    scale = dim ** (-0.5)
    base2 = scale * math.log2(math.e)
    spans = logits.shape[1]
    span = tiles // spans

    small = [
        pltpu.make_async_copy(mask, mask_all, sem_m.at[0]),
        pltpu.make_async_copy(head_slot, slots, sem_m.at[1]),
    ]
    lower = lax.rem(lax.axis_index("slab"), 2) == 0
    places = (
        (mid, halo, own),
        (even, pl.multiple_of(jnp.where(lower, halo + own, 0), rows), halo),
        (odd, pl.multiple_of(jnp.where(lower, 0, halo + own), rows), halo),
    )
    large = [
        pltpu.make_async_copy(source, kv_all.at[:, pl.ds(start, size)], sem_kv.at[i])
        for i, (source, start, size) in enumerate(places)
    ]
    for copy in large + small:
        copy.start()
    for copy in large:
        copy.wait()

    for c in range(count):
        for u in range(spans):
            low = u * span * rows
            logits[c, u] = lax.dot_general(
                kv_all[c, low : low + (span - 1 + band) * rows, :],
                q_all[c, low : low + span * rows, :],
                (((1,), (1,)), ((), ())),
                preferred_element_type=jnp.float32,
            )

    for copy in small:
        copy.wait()
    invert(slots, head_of, used)

    for c in range(count):
        slot = me * capacity + first + c
        head = head_of[slot]
        valid = used[slot] > 0
        for t in range(tiles):
            u, w = t // span, t % span
            columns = slice(w * rows, (w + 1) * rows)
            allowed, highest = [], None
            for b in range(band):
                tile = tile_base + t + b - reach
                flag = mask_all[b, t, head]
                allowed.append((flag > 0) & (tile >= 0) & (tile < tiles_all))
                part = logits[c, u, (w + b) * rows : (w + b + 1) * rows, columns]
                part = jnp.max(part.reshape(rows // 8, 8, rows), axis=0)
                part = jnp.where(allowed[b], part, -1e30)
                highest = part if highest is None else jnp.maximum(highest, part)
            highest = jnp.max(highest, axis=0, keepdims=True)
            total = None
            for b in range(band):
                shift = jnp.where(allowed[b], highest * base2, 1e30)
                part = logits[c, u, (w + b) * rows : (w + b + 1) * rows, columns]
                part = jnp.exp2(part * base2 - shift)
                weights[c * tiles + t, b * rows : (b + 1) * rows, :] = part.astype(jnp.bfloat16)
                part = jnp.sum(part.reshape(rows // 8, 8, rows), axis=0)
                total = part if total is None else total + part
            total = jnp.sum(total, axis=0, keepdims=True)
            place = slice(t * rows, (t + 1) * rows)
            totals[c : c + 1, place] = total
            lse = highest * scale + jnp.log(total)
            lse_ref[c : c + 1, place] = jnp.where(valid, lse, 0.0)

    for c in range(count):
        for t in range(tiles):
            place = slice(t * rows, (t + 1) * rows)
            summed = lax.dot_general(
                kv_all[count + c, t * rows : (t + band) * rows, :],
                weights[c * tiles + t],
                (((0,), (0,)), ((), ())),
                preferred_element_type=jnp.float32,
            )
            o_all[c, place, :] = jnp.transpose(summed / totals[c : c + 1, place]).astype(
                jnp.bfloat16
            )

    for k in range(owners):
        place = pl.ds(pl.multiple_of(lax.rem(me + k, owners) * tok, tok), tok)
        outs[k][...] = o_all[:, place, :]


def attend(head_slot, mask, near, queries, us, owners, *sizes):
    capacity, first, count, tiles, tiles_all, band = sizes
    _, tok_slab, dim = queries.shape
    rows = tok_slab // tiles
    span = 2 if tiles % 2 == 0 else 1
    out = jax.ShapeDtypeStruct((count, tok_slab // owners, dim), jnp.bfloat16)
    extended = tok_slab + (band - 1) * rows
    slots = owners * capacity
    return pl.pallas_call(
        functools.partial(attend_kernel, owners, capacity, first, count, tiles, tiles_all, band),
        out_shape=[out] * owners + [jax.ShapeDtypeStruct((count, tok_slab), jnp.float32)],
        in_specs=[ANY] * 5 + [VMEM],
        out_specs=[VMEM] * (owners + 1),
        scratch_shapes=[
            pltpu.VMEM((2 * count, extended, dim), jnp.bfloat16),
            pltpu.VMEM((count, tok_slab, dim), jnp.bfloat16),
            pltpu.VMEM((count, tiles // span, (span - 1 + band) * rows, span * rows), jnp.float32),
            pltpu.VMEM((count * tiles, band * rows, rows), jnp.bfloat16),
            pltpu.VMEM((count, tok_slab), jnp.float32),
            pltpu.SMEM(mask.shape, jnp.int32),
            pltpu.SMEM(head_slot.shape, jnp.int32),
            pltpu.SMEM((slots,), jnp.int32),
            pltpu.SMEM((slots,), jnp.int32),
            pltpu.SemaphoreType.DMA((3,)),
            pltpu.SemaphoreType.DMA((2,)),
        ],
        cost_estimate=hint(us),
        compiler_params=LARGE,
        name="attend",
    )(in_hbm(head_slot), in_hbm(mask), *near, queries)


def unpack_kernel(owners, capacity, first, count, dim, head_slot, *refs):
    blocks = refs[:owners]
    out, head_of, used, sem = refs[-4:]
    me = lax.axis_index("head")
    whole = owners * capacity == head_slot.shape[0]
    invert(head_slot, head_of, None if whole else used)

    def each(act):
        for k in range(owners):
            owner = lax.rem(me - k + owners, owners)
            for c in range(count):
                slot = owner * capacity + first + c
                columns = pl.ds(pl.multiple_of(head_of[slot] * dim, dim), dim)
                copy = pltpu.make_async_copy(
                    blocks[k].at[c], out.at[:, columns], sem.at[k * count + c]
                )
                if whole:
                    act(copy)
                else:
                    pl.when(used[slot] > 0)(functools.partial(act, copy))

    each(lambda copy: copy.start())
    each(lambda copy: copy.wait())


def unpack(head_slot, blocks, target, capacity, first, shape, us):
    owners = len(blocks)
    count, tok, dim = blocks[0].shape
    operands = list(blocks) + ([] if target is None else [target])
    return pl.pallas_call(
        functools.partial(unpack_kernel, owners, capacity, first, count, dim),
        out_shape=shape,
        in_specs=[SMEM] + [ANY] * owners + ([] if target is None else [HBM]),
        out_specs=HBM,
        input_output_aliases={} if target is None else {owners + 1: 0},
        scratch_shapes=[
            pltpu.SMEM((owners * capacity,), jnp.int32),
            pltpu.SMEM((owners * capacity,), jnp.int32),
            pltpu.SemaphoreType.DMA((owners * count,)),
        ],
        cost_estimate=hint(us),
        compiler_params=SMALL,
        name="unpack",
    )(head_slot, *operands)


def exchange(blocks):
    owners = len(blocks)
    order = ORDER if len(ORDER) == owners - 1 else range(1, owners)
    moved = {
        k: lax.ppermute(blocks[k], "head", [(i, (i + k) % owners) for i in range(owners)])
        for k in order
    }
    return [blocks[0]] + [moved[k] for k in range(1, owners)]


def swap(mid, parity, halo):
    slabs, length = lax.axis_size("slab"), mid.shape[1]
    pairs = [(i, i + 1) for i in range(parity, slabs - 1, 2)]
    if halo < length:
        lower = lax.rem(lax.axis_index("slab"), 2) == parity
        start = jnp.where(lower, length - halo, 0)
        mid = lax.dynamic_slice_in_dim(mid, start, halo, 1)
    return lax.ppermute(mid, "slab", pairs + [(j, i) for i, j in pairs])


def after(x, done):
    return pl.pallas_call(
        lambda *refs: None,
        out_shape=jax.ShapeDtypeStruct(x.shape, x.dtype),
        in_specs=[ANY, ANY],
        out_specs=ANY,
        input_output_aliases={0: 0},
        cost_estimate=hint(0.0),
        compiler_params=SMALL,
        name="after",
    )(x, done)


def on_device(query_rows, key_rows, value_rows, tile_mask, head_slot):
    owners = lax.axis_size("head")
    slabs = lax.axis_size("slab")
    tok_dev, width = query_rows.shape
    heads, tiles, band = tile_mask.shape
    dim = width // heads
    capacity = (heads + owners - 1) // owners
    tok_slab = tok_dev * owners
    halo = (band - 1) // 2 * (tok_slab // tiles)
    mask = jnp.transpose(tile_mask, (2, 1, 0))
    half = (SPLIT * capacity + 9) // 10
    groups = ((0, half), (half, capacity - half))
    source = {"q": query_rows, "k": key_rows, "v": value_rows}

    sizes = [[(name, *groups[g]) for name, g in held] for held in STAGES]
    args = (owners, capacity, dim)
    packed = pack(head_slot, source, sizes[:1], *args, PACK_US[0])
    if len(sizes) > 1:
        packed += pack(head_slot, source, sizes[1:], *args, PACK_US[1], packed[0][:1])
    moved = [exchange(blocks) for blocks in packed]
    near, queries = {}, {}
    for blocks, held in zip(moved, STAGES):
        skip = 0
        for name, g in held:
            count = groups[g][1]
            if name == "q":
                queries[g] = join(blocks, skip, count, QJOIN_US[g])
            if name == "k":
                mid = join(blocks, skip, 2 * count, JOIN_US[g])
                lead = FIRST[g]
                one = swap(mid, lead, halo)
                mid = after(mid, one)
                two = swap(mid, 1 - lead, halo)
                near[g] = (mid, two, one) if lead else (mid, one, two)
            skip += count

    target, lses = None, []
    for g, (first, count) in enumerate(groups):
        sizes = (owners, capacity, first, count, tiles, tiles * slabs, band)
        *outs, lse = attend(head_slot, mask, near[g], queries[g], ATTEND_US[g], *sizes)
        lses.append(lse)
        shape = jax.ShapeDtypeStruct(query_rows.shape, query_rows.dtype)
        target = unpack(head_slot, exchange(outs), target, capacity, first, shape, UNPACK_US[g])
    return target, jnp.concatenate(lses, axis=0)


def solution(mesh):
    rows = P(("groups", "slab", "head"), None)
    in_specs = (rows, rows, rows, P(None, ("groups", "slab"), None), P())
    out_specs = (rows, P("head", ("groups", "slab")))
    return jax.shard_map(
        on_device, mesh=mesh, in_specs=in_specs, out_specs=out_specs, check_vma=False
    )
```
